512 devices in a mesh: rep: 64 (over x, y, core), fsdp: 8 (over z).
Axes of the slice: x: 4, y: 8, z: 8, core: 2. Of those that a mesh axis runs over, the one named last changes fastest.
Arguments:
- base_weight: bfloat16 [32, 28672], P('fsdp'), may hold values from -6 to 6
- local_weight: bfloat16 [64, 32, 28672], P('rep', 'fsdp'), may hold values from -42 to 42
- momentum: float32 [32, 28672], P('fsdp'), may hold values from -3 to 3
Outputs:
- new_base: bfloat16 [32, 28672], replicated
- new_momentum: float32 [32, 28672], P('fsdp')
The draws below stay inside these ranges and needn't reach their ends.
All inputs are finite; a program needn't handle non-finite values.
Results may differ from the reference program's by a relative error of at most 0.0027.
Values may be sent and summed in bfloat16 or wider, within the bound.
A program may use at most 128 MiB of HBM per device.

```python
import jax
import jax.numpy as jnp
from jax import lax

FF = 28672
ROWS = 32
REPLICAS = 64


def shared_base(key):
    return jnp.clip(jax.random.normal(key, (ROWS, FF), jnp.float32), -6.0, 6.0)


def draw_base_weight(key, part):
    base = shared_base(key)
    return base.astype(jnp.bfloat16)


def draw_local_weight(key, part):
    base = shared_base(key)
    key = jax.random.fold_in(key, 7)
    noise_key, perm_key, rate_key = jax.random.split(key, 3)
    noise = jnp.clip(jax.random.normal(noise_key, (REPLICAS, ROWS, FF), jnp.float32), -3.0, 3.0)
    owner = jax.random.permutation(perm_key, REPLICAS)
    blocks = jnp.arange(FF) // (FF // REPLICAS)
    spiked = (blocks[None, :] == owner[:, None]).astype(jnp.float32)
    rates = jax.random.uniform(rate_key, (REPLICAS, 1, 1), jnp.float32, 0.5, 1.5)
    drift = noise * rates * (1.0 + 7.0 * spiked[:, None, :])
    return (base[None] - drift).astype(jnp.bfloat16)


def steps_of(own_key, dims, cuts, least, top_value):
    level, own = 1.0, jax.random.fold_in(own_key, 6)
    for position, shards_of in cuts:
        heights = jnp.exp(jax.random.uniform(jax.random.fold_in(own, position), (shards_of,), jnp.float32, least / len(cuts), top_value / len(cuts)))
        level = level * jnp.repeat(heights, dims[position] // shards_of).reshape([-1 if axis == position else 1 for axis in range(len(dims))])
    return level


def bell_draw(key, extent, width, most, cuts=(), held_as=jnp.bfloat16):
    gain = steps_of(key, extent, cuts, -0.22, 0.18) if cuts else 1.0
    values = jax.random.normal(key, extent, jnp.float32) * width * gain
    return jnp.minimum(jnp.maximum(values, -most), most).astype(held_as)


def setup_inputs(seed: int = 0) -> dict:
    key_of = jax.random.split(jax.random.key(seed), 4)
    base_weight = draw_base_weight(jax.random.fold_in(key_of[3], 71), 0)
    local_weight = draw_local_weight(jax.random.fold_in(key_of[3], 71), 0)
    momentum = bell_draw(key_of[2], (ROWS, FF), 0.5, 3.0, ((0, 8),), jnp.float32)
    return dict(base_weight=base_weight, local_weight=local_weight, momentum=momentum)


def reference(base_weight, local_weight, momentum):
    base_f = base_weight.astype(jnp.float32)
    delta = (base_f[None] - local_weight.astype(jnp.float32)).astype(jnp.bfloat16)
    delta = lax.optimization_barrier(delta)
    outer_grad = jnp.sum(delta.astype(jnp.float32), axis=0) / REPLICAS
    new_momentum = 0.9 * momentum + outer_grad
    new_base = (base_f - 0.7 * (outer_grad + 0.9 * new_momentum)).astype(jnp.bfloat16)
    return new_base, new_momentum
```

```python
import jax
import jax.numpy as jnp
from jax import lax
from jax.experimental import pallas as pl
from jax.experimental.pallas import tpu as pltpu
from jax.sharding import PartitionSpec as P

FF = 28672
NX, NY, NZ = 4, 8, 8
G = NX * 2
SEG = FF // G
PAIR = SEG // (NY // 2)
WIDE, SHIFT, NARROW = 512, 384, 384
f32, bf16 = jnp.float32, jnp.bfloat16


def kernel(base_h, local_h, mom_h, newb_h, newm_h, base_v, local_v, mom_v, send1, recv1, part, recv2, own_nb, zbuf,
           gath, nm, in_sem, out_sem, ssem, r1, r2, rz, ry_m, ry_b, rx_m, rx_b, rc_m, rc_b):
    rep = lax.axis_index("rep")
    z = lax.axis_index("fsdp")
    x = rep // (2 * NY)
    y = (rep // 2) % NY
    c = rep % 2
    g = x * 2 + c
    odd = y % 2

    def at(x_, y_, c_, z_):
        return {"rep": (x_ * NY + y_) * 2 + c_, "fsdp": z_}

    def g_peer(k):
        h = (g + k) % G
        return h, at(h // 2, y, h % 2, z)

    def y_peer(k):
        h = (y + k) % NY
        return h, at(x, h, c, z)

    def z_peer(k):
        h = (z + k) % NZ
        return h, at(x, y, c, h)

    barrier = pltpu.get_barrier_semaphore()
    for k in range(1, 8):
        for dev in (g_peer(k)[1], y_peer(k)[1], z_peer(k)[1]):
            pl.semaphore_signal(barrier, inc=1, device_id=dev, device_id_type=pl.DeviceIdType.MESH)

    def remote(src, dst, send, recv, dev):
        copy = pltpu.make_async_remote_copy(src_ref=src, dst_ref=dst, send_sem=send, recv_sem=recv, device_id=dev,
                                            device_id_type=pl.DeviceIdType.MESH)
        copy.start()

    def drain(ref, sem):
        pltpu.make_async_copy(ref, ref, sem).wait()

    def window(h, j):
        return pl.multiple_of(h * SEG + (j // 2) * PAIR + (j % 2) * SHIFT, 128)

    col = window(g, y)
    in_base = pltpu.make_async_copy(base_h, base_v, in_sem.at[0])
    in_local = pltpu.make_async_copy(local_h.at[0], local_v, in_sem.at[1])
    in_mom = pltpu.make_async_copy(mom_h.at[:, pl.ds(col, WIDE)], mom_v, in_sem.at[2])
    in_local.start()
    in_base.start()
    in_mom.start()
    in_local.wait()
    in_base.wait()

    for k in list(range(1, 8)) + [0]:
        h, dev = g_peer(k)
        cols = pl.ds(pl.multiple_of(h * SEG, 128), SEG)
        send1[k] = (base_v[:, cols].astype(f32) - local_v[:, cols].astype(f32)).astype(bf16)
        if k == 1:
            pl.semaphore_wait(barrier, 21)
        if k:
            remote(send1.at[k], recv1.at[k - 1], ssem.at[0], r1, dev)
    drain(recv1, r1)
    total = send1[0].astype(f32)
    for k in range(7):
        total += recv1[k].astype(f32)
    part[...] = total
    for k in range(1, 8):
        j, dev = y_peer(k)
        lo = pl.multiple_of((j // 2) * PAIR + (j % 2) * SHIFT, 128)
        remote(part.at[:, pl.ds(lo, WIDE)], recv2.at[k - 1], ssem.at[1], r2, dev)
    in_mom.wait()
    mine = pl.multiple_of((y // 2) * PAIR + odd * SHIFT, 128)
    total = part[:, pl.ds(mine, WIDE)]
    drain(recv2, r2)
    for k in range(7):
        total += recv2[k]
    grad = total * (1.0 / 64.0)
    new_m = 0.9 * mom_v[...] + grad
    b = base_v[:, pl.ds(col, WIDE)].astype(f32)
    new_b = (b - 0.7 * (grad + 0.9 * new_m)).astype(bf16)
    own_nb[...] = new_b
    for k in range(1, 8):
        _, dev = z_peer(k)
        remote(own_nb, zbuf.at[z], ssem.at[2], rz, dev)

    even_cols = pl.ds(col, WIDE)
    odd_cols = pl.ds(pl.multiple_of(col + 128, 128), NARROW)

    @pl.when(odd == 0)
    def _():
        nm[:, even_cols] = new_m
        for k in range(1, 8):
            remote(nm.at[:, even_cols], nm.at[:, even_cols], ssem.at[3], ry_m, y_peer(k)[1])

    @pl.when(odd == 1)
    def _():
        nm[:, odd_cols] = new_m[:, 128:]
        for k in range(1, 8):
            remote(nm.at[:, odd_cols], nm.at[:, odd_cols], ssem.at[3], ry_m, y_peer(k)[1])

    drain(zbuf.at[pl.ds(0, 7)], rz)
    zbuf[z] = new_b
    slab = jnp.concatenate([zbuf[i].astype(f32) for i in range(NZ)], axis=0).astype(bf16)

    @pl.when(odd == 0)
    def _():
        gath[:, even_cols] = slab
        for k in range(1, 8):
            remote(gath.at[:, even_cols], gath.at[:, even_cols], ssem.at[4], ry_b, y_peer(k)[1])

    @pl.when(odd == 1)
    def _():
        gath[:, odd_cols] = slab[:, 128:]
        for k in range(1, 8):
            remote(gath.at[:, odd_cols], gath.at[:, odd_cols], ssem.at[4], ry_b, y_peer(k)[1])

    n_even = SEG - WIDE
    n_odd = SEG - NARROW

    def drain_y(buf, sem):
        @pl.when(odd == 0)
        def _():
            drain(buf.at[:, pl.ds(0, n_even)], sem)

        @pl.when(odd == 1)
        def _():
            drain(buf.at[:, pl.ds(0, n_odd)], sem)

    def seg(buf, h):
        return buf.at[:, pl.ds(pl.multiple_of(h * SEG, 128), SEG)]

    partner = at(x, y, 1 - c, z)

    def spread(buf, sems, send):
        for k in (1, 3, 2):
            dev = at((x + k) % NX, y, c, z)
            remote(seg(buf, g), seg(buf, g), send, sems.at[k - 1], dev)

    drain_y(nm, ry_m)
    spread(nm, rx_m, ssem.at[5])
    remote(seg(nm, g), seg(nm, g), ssem.at[6], rc_m.at[0], partner)
    drain_y(gath, ry_b)
    spread(gath, rx_b, ssem.at[7])
    remote(seg(gath, g), seg(gath, g), ssem.at[8], rc_b.at[0], partner)

    for buf, rx, rc, send in ((nm, rx_m, rc_m, ssem.at[6]), (gath, rx_b, rc_b, ssem.at[8])):
        for k in (1, 3, 2):
            h = ((x - k) % NX) * 2 + c
            drain(seg(buf, h), rx.at[k - 1])
            remote(seg(buf, h), seg(buf, h), send, rc.at[k], partner)
    for buf, rc in ((nm, rc_m), (gath, rc_b)):
        for k in range(4):
            drain(seg(buf, 0), rc.at[k])
    out_m = pltpu.make_async_copy(nm, newm_h, out_sem.at[0])
    out_b = pltpu.make_async_copy(gath, newb_h, out_sem.at[1])
    out_m.start()
    out_b.start()
    drain(recv1, ssem.at[0])
    drain(recv2, ssem.at[1])
    drain(zbuf.at[pl.ds(0, 7)], ssem.at[2])

    @pl.when(odd == 0)
    def _():
        drain(nm.at[:, pl.ds(0, 7 * WIDE)], ssem.at[3])
        drain(gath.at[:, pl.ds(0, 7 * WIDE)], ssem.at[4])

    @pl.when(odd == 1)
    def _():
        drain(nm.at[:, pl.ds(0, 7 * NARROW)], ssem.at[3])
        drain(gath.at[:, pl.ds(0, 7 * NARROW)], ssem.at[4])

    drain(nm.at[:, pl.ds(0, 3 * SEG)], ssem.at[5])
    drain(nm.at[:, pl.ds(0, 4 * SEG)], ssem.at[6])
    drain(gath.at[:, pl.ds(0, 3 * SEG)], ssem.at[7])
    drain(gath.at[:, pl.ds(0, 4 * SEG)], ssem.at[8])
    out_m.wait()
    out_b.wait()


def shards(base_weight, local_weight, momentum):
    any_ = pl.BlockSpec(memory_space=pl.ANY)
    dma = pltpu.SemaphoreType.DMA
    return pl.pallas_call(
        kernel,
        out_shape=(jax.ShapeDtypeStruct((32, FF), bf16), jax.ShapeDtypeStruct((4, FF), f32)),
        in_specs=[any_] * 3,
        out_specs=(any_, any_),
        scratch_shapes=[
            pltpu.VMEM((4, FF), bf16),
            pltpu.VMEM((4, FF), bf16),
            pltpu.VMEM((4, WIDE), f32),
            pltpu.VMEM((8, 4, SEG), bf16),
            pltpu.VMEM((7, 4, SEG), bf16),
            pltpu.VMEM((4, SEG), f32),
            pltpu.VMEM((7, 4, WIDE), f32),
            pltpu.VMEM((4, WIDE), bf16),
            pltpu.VMEM((8, 4, WIDE), bf16),
            pltpu.VMEM((32, FF), bf16),
            pltpu.VMEM((4, FF), f32),
            dma((3,)),
            dma((2,)),
            dma((9,)),
            dma, dma, dma, dma, dma,
            dma((3,)), dma((3,)), dma((4,)), dma((4,)),
        ],
        compiler_params=pltpu.CompilerParams(collective_id=0, has_side_effects=True, vmem_limit_bytes=32 * 2**20),
        cost_estimate=pl.CostEstimate(flops=4 * FF * 8, bytes_accessed=32 * FF * 4, transcendentals=0),
    )(base_weight, local_weight, momentum)


def solution(mesh):
    return jax.shard_map(
        shards,
        mesh=mesh,
        in_specs=(P("fsdp", None), P("rep", "fsdp", None), P("fsdp", None)),
        out_specs=(P(), P("fsdp", None)),
        check_vma=False,
    )
```

```python
import jax
import jax.numpy as jnp
from jax import lax
from jax.experimental import pallas as pl
from jax.experimental.pallas import tpu as pltpu
from jax.sharding import PartitionSpec as P

FF = 28672
NX, NY, NZ = 4, 8, 8
G = NX * 2
BLOCK = FF // NY
CHIP = BLOCK // NX
WIDE, NARROW = 512, 384
SUM_SLOTS = (4, 3, -3, 2, -2, 1, -1, 0)
SLOTS = (0, 1, -1, 2, -2, 3, -3, 4)
GROUPS = ((0, 1), (1, 2), (3, 2), (5, 3))
f32, bf16 = jnp.float32, jnp.bfloat16
MESH = pl.DeviceIdType.MESH


def slot_of(offset):
    return SLOTS.index((offset + 3) % NY - 3)


def place():
    rep = lax.axis_index("rep")
    return rep // (2 * NY), (rep // 2) % NY, rep % 2, lax.axis_index("fsdp")


def kernel(base_h, local_h, mom_h, gath, gath_m, base_v, local_v, mom_v, send1, recv1, part, recv2, own_nb, zbuf,
           in_sem, s1, s2, sz, sy_m, sy_b, sx_m, sx_b, sc_m, sc_b, r1, r2, rz, ry_m, ry_b, rx_m, rx_b, rh_b, rc_m, rc_b):
    x, y, c, z = place()

    def at(x_, y_, c_, z_):
        return {"rep": (x_ * NY + y_) * 2 + c_, "fsdp": z_}

    def g_peer(k):
        h = (x * 2 + c + k) % G
        return h // 2, h % 2

    def y_peer(k):
        return at(x, (y + k) % NY, c, z)

    def x_peer(k):
        return at((x + k) % NX, y, c, z)

    partner = at(x, y, 1 - c, z)
    barrier = pltpu.get_barrier_semaphore()
    for k in range(1, 8):
        gx, gc = g_peer(k)
        for dev in (at(gx, y, gc, z), y_peer(k), at(x, y, c, (z + k) % NZ)):
            pl.semaphore_signal(barrier, inc=1, device_id=dev, device_id_type=MESH)

    def remote(src, dst, send, recv, dev):
        pltpu.make_async_remote_copy(src_ref=src, dst_ref=dst, send_sem=send, recv_sem=recv, device_id=dev,
                                     device_id_type=MESH).start()

    def drain(ref, sem):
        pltpu.make_async_copy(ref, ref, sem).wait()

    def window(j, x_, c_):
        return pl.ds(pl.multiple_of(j * BLOCK + x_ * CHIP + c_ * NARROW, 128), WIDE)

    mine = window(y, x, c)
    in_local = pltpu.make_async_copy(local_h.at[0], local_v, in_sem.at[0])
    in_base = pltpu.make_async_copy(base_h, base_v, in_sem.at[1])
    in_mom = pltpu.make_async_copy(mom_h.at[:, mine], mom_v, in_sem.at[2])
    in_local.start()
    in_base.start()
    in_mom.start()
    in_local.wait()
    in_base.wait()

    for half in range(2):
        for k in list(range(1, 8)) + [0]:
            gx, gc = g_peer(k)
            for i in range(4):
                cols = window((y + SUM_SLOTS[half * 4 + i]) % NY, gx, gc)
                send1[half, k, i] = (base_v[:, cols].astype(f32) - local_v[:, cols].astype(f32)).astype(bf16)
            if half == 0 and k == 1:
                pl.semaphore_wait(barrier, 21)
            if k:
                remote(send1.at[half, k], recv1.at[half, k - 1], s1, r1.at[half], at(gx, y, gc, z))
    for half in range(2):
        drain(recv1.at[half], r1.at[half])
        for i in range(4):
            total = send1[half, 0, i].astype(f32)
            for k in range(7):
                total += recv1[half, k, i].astype(f32)
            part[half * 4 + i] = total
            off = SUM_SLOTS[half * 4 + i]
            if off:
                remote(part.at[half * 4 + i], recv2.at[(off - 1) % NY], s2, r2, y_peer(off))
    total = part[7]
    in_mom.wait()
    b = base_v[:, mine].astype(f32)
    drain(recv2, r2)
    for k in range(7):
        total += recv2[k]
    grad = total * (1.0 / 64.0)
    new_m = 0.9 * mom_v[...] + grad
    new_b = (b - 0.7 * (grad + 0.9 * new_m)).astype(bf16)
    own_nb[...] = new_b
    for k in range(1, 8):
        remote(own_nb, zbuf.at[z], sz, rz, at(x, y, c, (z + k) % NZ))
    zbuf[z] = new_b

    def gather(par):
        lo, w = (0, WIDE) if par == 0 else (128, NARROW)
        other = WIDE + NARROW - w

        def cols_of(x_):
            return pl.ds(pl.multiple_of(x_ * CHIP + par * WIDE, 128), w)

        own = cols_of(x)

        def blocks(buf, g, x_):
            return buf.at[pl.ds(*g), :, cols_of(x_)]

        def pass_on(buf, g, x_, send, recv):
            remote(blocks(buf, g, x_), blocks(buf, g, x_), send, recv, partner)

        gath_m[0, :, own] = new_m[:, lo:]
        for k in SLOTS[1:]:
            remote(gath_m.at[0, :, own], gath_m.at[slot_of(-k), :, own], sy_m, ry_m, y_peer(k))
        drain(zbuf.at[pl.ds(0, 7)], rz)
        slab = jnp.concatenate([zbuf[i][:, lo:].astype(f32) for i in range(NZ)], axis=0).astype(bf16)
        gath[0, :, own] = slab
        for k in SLOTS[1:]:
            slot = slot_of(-k)
            group = (slot + 1) // 2 if slot < 7 else 3
            remote(gath.at[0, :, own], gath.at[slot, :, own], sy_b, ry_b.at[group - 1], y_peer(k))
        every = (0, NY)

        def feed(i):
            g = GROUPS[i]
            if i:
                drain(blocks(gath, g, 0), ry_b.at[i - 1])
            for d, k in enumerate((1, -1)):
                remote(blocks(gath, g, x), blocks(gath, g, x), sx_b, rx_b.at[d, i], x_peer(k))
            pass_on(gath, g, x, sc_b, rc_b.at[0, i])

        def half_of(i, d, x_):
            return gath.at[pl.ds(*GROUPS[i]), pl.ds(d * 16, 16), cols_of(x_)]

        def take(i):
            for d, k in enumerate((1, -1)):
                from_ = (x - k) % NX
                drain(blocks(gath, GROUPS[i], 0), rx_b.at[d, i])
                remote(half_of(i, d, from_), half_of(i, d, from_), sx_b, rh_b.at[d, i], x_peer(k))
                pass_on(gath, GROUPS[i], from_, sc_b, rc_b.at[1 + d, i])

        feed(0)
        drain(gath_m.at[pl.ds(0, 7), :, cols_of(0)], ry_m)
        for k in (1, 3, 2):
            remote(blocks(gath_m, every, x), blocks(gath_m, every, x), sx_m, rx_m.at[k - 1], x_peer(k))
        pass_on(gath_m, every, x, sc_m, rc_m.at[0])
        feed(1)
        take(0)
        feed(2)
        for k in (1, 3, 2):
            drain(blocks(gath_m, every, 0), rx_m.at[k - 1])
            pass_on(gath_m, every, (x - k) % NX, sc_m, rc_m.at[k])
        take(1)
        feed(3)
        take(2)
        take(3)
        for i in range(4):
            for d in range(2):
                drain(half_of(i, d, 0), rh_b.at[d, i])
            pass_on(gath, GROUPS[i], (x + 2) % NX, sc_b, rc_b.at[3, i])
        drain(gath_m.at[pl.ds(0, 7), :, cols_of(0)], sy_m)
        drain(gath.at[pl.ds(0, 7), :, cols_of(0)], sy_b)
        drain(gath_m.at[:, :, pl.ds(0, 3 * w)], sx_m)
        drain(gath.at[:, :, pl.ds(0, 3 * w)], sx_b)
        drain(gath_m.at[:, :, pl.ds(0, 4 * w)], sc_m)
        drain(gath.at[:, :, pl.ds(0, 4 * w)], sc_b)
        for k in range(4):
            drain(gath_m.at[:, :, pl.ds(0, other)], rc_m.at[k])
            for i in range(4):
                drain(gath.at[pl.ds(*GROUPS[i]), :, pl.ds(0, other)], rc_b.at[k, i])

    for par in range(2):
        pl.when(c == par)(lambda par=par: gather(par))
    drain(recv1, s1)
    drain(recv2, s2)
    drain(zbuf.at[pl.ds(0, 7)], sz)


def flush_kernel(gath, gath_m, newb, newm, sem):
    y = place()[1]
    copies = []
    for s, off in enumerate(SLOTS):
        cols = pl.ds(pl.multiple_of((y + off) % NY * BLOCK, 128), BLOCK)
        copies.append(pltpu.make_async_copy(gath.at[s], newb.at[:, cols], sem.at[0, s]))
        copies.append(pltpu.make_async_copy(gath_m.at[s], newm.at[:, cols], sem.at[1, s]))
    for copy in copies:
        copy.start()
    for copy in copies:
        copy.wait()


def shards(base_weight, local_weight, momentum):
    hbm, vmem = pl.BlockSpec(memory_space=pltpu.HBM), pl.BlockSpec(memory_space=pltpu.VMEM)
    dma = pltpu.SemaphoreType.DMA
    gath, gath_m = pl.pallas_call(
        kernel,
        out_shape=(pltpu.VMEM((NY, 32, BLOCK), bf16), pltpu.VMEM((NY, 4, BLOCK), f32)),
        in_specs=[hbm] * 3,
        out_specs=(vmem, vmem),
        scratch_shapes=[
            pltpu.VMEM((4, FF), bf16),
            pltpu.VMEM((4, FF), bf16),
            pltpu.VMEM((4, WIDE), f32),
            pltpu.VMEM((2, 8, 4, 4, WIDE), bf16),
            pltpu.VMEM((2, 7, 4, 4, WIDE), bf16),
            pltpu.VMEM((8, 4, WIDE), f32),
            pltpu.VMEM((7, 4, WIDE), f32),
            pltpu.VMEM((4, WIDE), bf16),
            pltpu.VMEM((8, 4, WIDE), bf16),
            dma((3,)),
            dma, dma, dma, dma, dma, dma, dma, dma, dma,
            dma((2,)), dma, dma, dma, dma((3,)), dma((3,)), dma((2, 4)), dma((2, 4)), dma((4,)), dma((4, 4)),
        ],
        compiler_params=pltpu.CompilerParams(collective_id=0, has_side_effects=True, vmem_limit_bytes=32 * 2**20),
        cost_estimate=pl.CostEstimate(flops=4 * FF * 8, bytes_accessed=32 * FF * 4, transcendentals=0),
    )(*(pltpu.with_memory_space_constraint(a, pltpu.HBM) for a in (base_weight, local_weight, momentum)))
    return pl.pallas_call(
        flush_kernel,
        out_shape=(pltpu.HBM((32, FF), bf16), pltpu.HBM((4, FF), f32)),
        in_specs=[vmem, vmem],
        out_specs=(hbm, hbm),
        scratch_shapes=[dma((2, NY))],
        cost_estimate=pl.CostEstimate(flops=0, bytes_accessed=32 * FF * 4, transcendentals=0),
    )(*(pltpu.with_memory_space_constraint(a, pltpu.VMEM) for a in (gath, gath_m)))


def solution(mesh):
    return jax.shard_map(
        shards,
        mesh=mesh,
        in_specs=(P("fsdp", None), P("rep", "fsdp", None), P("fsdp", None)),
        out_specs=(P(), P("fsdp", None)),
        check_vma=False,
    )
```

```python
import jax
import jax.numpy as jnp
from jax import lax
from jax.experimental import pallas as pl
from jax.experimental.pallas import tpu as pltpu
from jax.sharding import PartitionSpec as P

FF = 28672
NX, NY, NZ = 4, 8, 8
BLOCK = FF // NY
CHIP = BLOCK // NX
WIDE, NARROW = 512, 384
SLOTS = (0, 1, -1, 2, -2, 3, -3, 4)
GROUPS = ((0, 0, 1), (0, 1, 4), (0, 5, 3), (1, 0, 4), (1, 4, 4))
DIRECT = (3, 4)
PLANE = sorted(((i, j, k) for i in range(NX) for j in range(NY) for k in range(2)),
               key=lambda d: (-min(d[0], NX - d[0]) - min(d[1], NY - d[1]), -d[2]))
f32, bf16 = jnp.float32, jnp.bfloat16
MESH = pl.DeviceIdType.MESH


def slot_of(offset):
    return SLOTS.index((offset + 3) % NY - 3)


def place():
    rep = lax.axis_index("rep")
    return rep // (2 * NY), (rep // 2) % NY, rep % 2, lax.axis_index("fsdp")


def kernel(base_h, local_h, mom_h, gath, gath_m, base_v, local_v, mom_v, send1, recv1, own_a, own_c, abuf, bbuf,
           cbuf, in_sem, send_sem, r1, rz_a, ry_a, ry_b, rz_b, rx_c, rz_c, ry_c, ry_m, rx_m, rx, rh, rf, rc, rc_c, rc_m):
    x, y, c, z = place()
    s1, sz_a, sy_a, sy_b, sz_b, sx_c, sz_c, sy_c, sy_m, sx_m, sx, sc, sc_m = (send_sem.at[i] for i in range(13))

    def at(x_, y_, c_, z_):
        return {"rep": (x_ * NY + y_) * 2 + c_, "fsdp": z_}

    def y_peer(k):
        return at(x, (y + k) % NY, c, z)

    def z_peer(k):
        return at(x, y, c, (z + k) % NZ)

    def x_peer(k):
        return at((x + k) % NX, y, c, z)

    partner = at(x, y, 1 - c, z)
    barrier = pltpu.get_barrier_semaphore()
    for dx, dy, dc in PLANE[:-1]:
        dev = at((x + dx) % NX, (y + dy) % NY, (c + dc) % 2, z)
        pl.semaphore_signal(barrier, inc=1, device_id=dev, device_id_type=MESH)
    for k in range(1, NZ):
        pl.semaphore_signal(barrier, inc=1, device_id=z_peer(k), device_id_type=MESH)

    def remote(src, dst, send, recv, dev):
        pltpu.make_async_remote_copy(src_ref=src, dst_ref=dst, send_sem=send, recv_sem=recv, device_id=dev,
                                     device_id_type=MESH).start()

    def drain(ref, sem):
        pltpu.make_async_copy(ref, ref, sem).wait()

    def window(j, x_, c_):
        return pl.ds(pl.multiple_of(j * BLOCK + x_ * CHIP + c_ * NARROW, 128), WIDE)

    mine = window(y, x, c)
    in_local = pltpu.make_async_copy(local_h.at[0], local_v, in_sem.at[0])
    in_base = pltpu.make_async_copy(base_h, base_v, in_sem.at[1])
    in_mom = pltpu.make_async_copy(mom_h.at[:, mine], mom_v, in_sem.at[2])
    in_local.start()
    in_base.start()
    in_mom.start()
    in_local.wait()
    in_base.wait()

    for k, (dx, dy, dc) in enumerate(PLANE):
        dev = (x + dx) % NX, (y + dy) % NY, (c + dc) % 2
        cols = window(dev[1], dev[0], dev[2])
        send1[k] = (base_v[:, cols].astype(f32) - local_v[:, cols].astype(f32)).astype(bf16)
        if k == 0:
            pl.semaphore_wait(barrier, len(PLANE) - 1 + NZ - 1)
        if k < 63:
            remote(send1.at[k], recv1.at[k], s1, r1.at[k // 32], at(*dev, z))
    total = send1[63].astype(f32)
    in_mom.wait()
    b = base_v[:, mine].astype(f32)
    for part in (range(32), range(32, 63)):
        drain(recv1.at[pl.ds(0, len(part))], r1.at[part[0] // 32])
        for k in part:
            total += recv1[k].astype(f32)
    grad = total * (1.0 / 64.0)
    new_m = 0.9 * mom_v[...] + grad
    new_b = (b - 0.7 * (grad + 0.9 * new_m)).astype(bf16)
    own_a[...] = new_b[:, :256]
    own_c[...] = new_b[:, 384:]
    abuf[z] = new_b[:, :256]
    bbuf[z, 0] = new_b[:, 256:384]
    cbuf[z, x] = new_b[:, 384:]
    for k in (2, 1, 3):
        remote(own_c, cbuf.at[z, x], sx_c, rx_c, x_peer(k))
    for k in SLOTS[:0:-1]:
        remote(own_a, abuf.at[z], sz_a, rz_a, z_peer(k))
        remote(bbuf.at[z, 0], bbuf.at[z, slot_of(-k)], sy_b, ry_b, y_peer(k))

    def rows(parts):
        return jnp.concatenate([p.astype(f32) for p in parts], axis=0).astype(bf16)

    def gather(par):
        lo, w = (0, WIDE) if par == 0 else (128, NARROW)
        other = WIDE + NARROW - w
        w_a = 256 - lo
        own = pl.ds(par * WIDE, w)
        cols = (pl.ds(par * WIDE, w_a), pl.ds(par * WIDE + w_a, 128), pl.ds(par * WIDE + w_a + 128, 128))

        def blocks(i, x_):
            part_, start, n = GROUPS[i]
            return gath.at[pl.ds(start, n), x_, :, cols[part_]]

        def halves(i, d, x_):
            part_, start, n = GROUPS[i]
            return gath.at[pl.ds(start, n), x_, pl.ds(d * 16, 16), cols[part_]]

        def pass_on(i, x_, k):
            remote(blocks(i, x_), blocks(i, x_), sc, rc.at[k, i], partner)

        def feed(i):
            if i in DIRECT:
                remote(blocks(i, x), blocks(i, x), sx, rf.at[i], x_peer(2))
            for d, k in enumerate((1, -1)):
                remote(blocks(i, x), blocks(i, x), sx, rx.at[d, i], x_peer(k))
            pass_on(i, x, 0)

        def take(i):
            for d, k in enumerate((1, -1)):
                from_ = (x - k) % NX
                drain(blocks(i, 0), rx.at[d, i])
                if i not in DIRECT:
                    remote(halves(i, d, from_), halves(i, d, from_), sx, rh.at[d, i], x_peer(k))
                pass_on(i, from_, 1 + d)

        def far(i):
            if i in DIRECT:
                drain(blocks(i, 0), rf.at[i])
            else:
                for d in range(2):
                    drain(halves(i, d, 0), rh.at[d, i])
            pass_on(i, (x + 2) % NX, 3)

        def momentum(x_):
            return gath_m.at[:, x_, :, own]

        gath_m[0, x, :, own] = new_m[:, lo:]
        for k in SLOTS[:0:-1]:
            remote(gath_m.at[0, x, :, own], gath_m.at[slot_of(-k), x, :, own], sy_m, ry_m, y_peer(k))
        drain(cbuf.at[0, pl.ds(0, 3)], rx_c)
        for k in SLOTS[:0:-1]:
            remote(cbuf.at[z], cbuf.at[z], sz_c, rz_c, z_peer(k))
        drain(abuf.at[pl.ds(0, 7)], rz_a)
        gath[0, x, :, cols[0]] = rows([abuf[i][:, lo:] for i in range(NZ)])
        for k in SLOTS[1:]:
            slot = slot_of(-k)
            remote(gath.at[0, x, :, cols[0]], gath.at[slot, x, :, cols[0]], sy_a, ry_a.at[int(slot > 4)], y_peer(k))
        drain(bbuf.at[0, pl.ds(0, 7)], ry_b)
        for k in SLOTS[:0:-1]:
            remote(bbuf.at[z], bbuf.at[z], sz_b, rz_b, z_peer(k))
        feed(0)
        drain(gath_m.at[pl.ds(0, 7), 0, :, own], ry_m)
        for k in (2, 1, 3):
            remote(momentum(x), momentum(x), sx_m, rx_m.at[k - 1], x_peer(k))
        remote(momentum(x), momentum(x), sc_m, rc_m.at[0], partner)
        drain(cbuf.at[pl.ds(0, 7)], rz_c)
        for i in range(NX):
            gath[0, i, :, cols[2]] = rows([cbuf[j, i] for j in range(NZ)])
        for k in SLOTS[:0:-1]:
            slot = slot_of(-k)
            remote(gath.at[0, :, :, cols[2]], gath.at[slot, :, :, cols[2]], sy_c, ry_c.at[int(slot > 4)], y_peer(k))
        remote(gath.at[0, :, :, cols[2]], gath.at[0, :, :, cols[2]], sc, rc_c.at[0], partner)
        drain(blocks(1, 0), ry_a.at[0])
        feed(1)
        take(0)
        drain(blocks(2, 0), ry_a.at[1])
        feed(2)
        drain(bbuf.at[pl.ds(0, 7)], rz_b)
        for s in range(NY):
            gath[s, x, :, cols[1]] = rows([bbuf[i, s] for i in range(NZ)])
            if s == 3:
                feed(3)
        feed(4)
        take(1)
        for k in (1, 3, 2):
            drain(momentum(0), rx_m.at[k - 1])
            remote(momentum((x - k) % NX), momentum((x - k) % NX), sc_m, rc_m.at[k], partner)
        far(0)
        take(2)
        take(3)
        take(4)
        for i, near in ((1, pl.ds(1, 4)), (2, pl.ds(5, 3))):
            far(i)
            block = gath.at[near, :, :, cols[2]]
            drain(block, ry_c.at[i - 1])
            remote(block, block, sc, rc_c.at[i], partner)
        far(3)
        far(4)
        drain(gath_m.at[pl.ds(0, 7), 0, :, own], sy_m)
        drain(gath.at[pl.ds(0, 7), 0, :, cols[0]], sy_a)
        drain(gath.at[pl.ds(0, 7), :, :, cols[2]], sy_c)
        drain(gath_m.at[:, pl.ds(0, 3), :, own], sx_m)
        drain(gath_m.at[:, :, :, own], sc_m)
        drain(gath.at[:, pl.ds(0, 3), :, pl.ds(0, w_a + 128)], sx)
        drain(gath.at[:, :, :, own], sc)
        for k in range(4):
            drain(gath_m.at[:, 0, :, pl.ds(0, other)], rc_m.at[k])
            for i, (part_, start, n) in enumerate(GROUPS):
                drain(gath.at[pl.ds(start, n), 0, :, pl.ds(0, 128 if part_ else other - 256)], rc.at[k, i])
        for i, n in enumerate((1, 4, 3)):
            drain(gath.at[pl.ds(0, n), :, :, pl.ds(0, 128)], rc_c.at[i])

    for par in range(2):
        pl.when(c == par)(lambda par=par: gather(par))
    drain(recv1, s1)
    drain(abuf.at[pl.ds(0, 7)], sz_a)
    drain(bbuf.at[0, pl.ds(0, 7)], sy_b)
    drain(bbuf.at[pl.ds(0, 7)], sz_b)
    drain(cbuf.at[0, pl.ds(0, 3)], sx_c)
    drain(cbuf.at[pl.ds(0, 7)], sz_c)


def flush_kernel(gath, gath_m, newb, newm, sem):
    y = place()[1]
    copies = []
    for s, off in enumerate(SLOTS):
        for i in range(NX):
            cols = pl.ds(pl.multiple_of((y + off) % NY * BLOCK + i * CHIP, 128), CHIP)
            copies.append(pltpu.make_async_copy(gath.at[s, i], newb.at[:, cols], sem.at[0, s, i]))
            copies.append(pltpu.make_async_copy(gath_m.at[s, i], newm.at[:, cols], sem.at[1, s, i]))
    for copy in copies:
        copy.start()
    for copy in copies:
        copy.wait()


def shards(base_weight, local_weight, momentum):
    hbm, vmem = pl.BlockSpec(memory_space=pltpu.HBM), pl.BlockSpec(memory_space=pltpu.VMEM)
    dma = pltpu.SemaphoreType.DMA
    gath, gath_m = pl.pallas_call(
        kernel,
        out_shape=(pltpu.VMEM((NY, NX, 32, CHIP), bf16), pltpu.VMEM((NY, NX, 4, CHIP), f32)),
        in_specs=[hbm] * 3,
        out_specs=(vmem, vmem),
        scratch_shapes=[
            pltpu.VMEM((4, FF), bf16),
            pltpu.VMEM((4, FF), bf16),
            pltpu.VMEM((4, WIDE), f32),
            pltpu.VMEM((64, 4, WIDE), bf16),
            pltpu.VMEM((63, 4, WIDE), bf16),
            pltpu.VMEM((4, 256), bf16),
            pltpu.VMEM((4, 128), bf16),
            pltpu.VMEM((NZ, 4, 256), bf16),
            pltpu.VMEM((NZ, NY, 4, 128), bf16),
            pltpu.VMEM((NZ, NX, 4, 128), bf16),
            dma((3,)),
            dma((13,)),
            dma((2,)), dma, dma((2,)), dma, dma, dma, dma, dma((2,)), dma, dma((3,)),
            dma((2, 5)), dma((2, 5)), dma((5,)), dma((4, 5)), dma((3,)), dma((4,)),
        ],
        compiler_params=pltpu.CompilerParams(collective_id=0, has_side_effects=True, vmem_limit_bytes=32 * 2**20),
        cost_estimate=pl.CostEstimate(flops=4 * FF * 8, bytes_accessed=32 * FF * 4, transcendentals=0),
    )(*(pltpu.with_memory_space_constraint(a, pltpu.HBM) for a in (base_weight, local_weight, momentum)))
    return pl.pallas_call(
        flush_kernel,
        out_shape=(pltpu.HBM((32, FF), bf16), pltpu.HBM((4, FF), f32)),
        in_specs=[vmem, vmem],
        out_specs=(hbm, hbm),
        scratch_shapes=[dma((2, NY, NX))],
        cost_estimate=pl.CostEstimate(flops=0, bytes_accessed=32 * FF * 4, transcendentals=0),
    )(*(pltpu.with_memory_space_constraint(a, pltpu.VMEM) for a in (gath, gath_m)))


def solution(mesh):
    return jax.shard_map(
        shards,
        mesh=mesh,
        in_specs=(P("fsdp", None), P("rep", "fsdp", None), P("fsdp", None)),
        out_specs=(P(), P("fsdp", None)),
        check_vma=False,
    )
```

```python
import jax
import jax.numpy as jnp
from jax import lax
from jax.experimental import pallas as pl
from jax.experimental.pallas import tpu as pltpu
from jax.sharding import PartitionSpec as P

FF = 28672
NX, NY, NZ = 4, 8, 8
BLOCK = FF // NY
CHIP = BLOCK // NX
WIDE, NARROW = 512, 384
SLOTS = (0, 1, -1, 2, -2, 3, -3, 4)
GROUPS = ((0, 1), (1, 2), (3, 2), (5, 3))
DIRECT = (3,)
PLANE = sorted(((i, j, k) for i in range(NX) for j in range(NY) for k in range(2)),
               key=lambda d: (-min(d[0], NX - d[0]) - min(d[1], NY - d[1]), -d[2]))
f32, bf16 = jnp.float32, jnp.bfloat16
MESH = pl.DeviceIdType.MESH


def slot_of(offset):
    return SLOTS.index((offset + 3) % NY - 3)


def place():
    rep = lax.axis_index("rep")
    return rep // (2 * NY), (rep // 2) % NY, rep % 2, lax.axis_index("fsdp")


def kernel(base_h, local_h, mom_h, gath, gath_m, base_v, local_v, mom_v, send1, recv1, own_a, own_c, abuf, bbuf,
           cbuf, in_sem, send_sem, r1, rz_a, ry_a, ry_b, rx_b, rz_b, rx_c, rz_c, ry_c, ry_m, rx_m, rx, rh, rf, rc, rc_b, rc_c,
           rc_m):
    x, y, c, z = place()
    s1, sz_a, sy_a, sy_b, sx_b, sz_b, sx_c, sz_c, sy_c, sy_m, sx_m, sx, sc, sc_m = (send_sem.at[i] for i in range(14))

    def at(x_, y_, c_, z_):
        return {"rep": (x_ * NY + y_) * 2 + c_, "fsdp": z_}

    def y_peer(k):
        return at(x, (y + k) % NY, c, z)

    def z_peer(k):
        return at(x, y, c, (z + k) % NZ)

    def x_peer(k):
        return at((x + k) % NX, y, c, z)

    partner = at(x, y, 1 - c, z)
    barrier = pltpu.get_barrier_semaphore()
    for dx, dy, dc in PLANE[:-1]:
        dev = at((x + dx) % NX, (y + dy) % NY, (c + dc) % 2, z)
        pl.semaphore_signal(barrier, inc=1, device_id=dev, device_id_type=MESH)
    for k in range(1, NZ):
        pl.semaphore_signal(barrier, inc=1, device_id=z_peer(k), device_id_type=MESH)

    def remote(src, dst, send, recv, dev):
        pltpu.make_async_remote_copy(src_ref=src, dst_ref=dst, send_sem=send, recv_sem=recv, device_id=dev,
                                     device_id_type=MESH).start()

    def drain(ref, sem):
        pltpu.make_async_copy(ref, ref, sem).wait()

    def window(j, x_, c_):
        return pl.ds(pl.multiple_of(j * BLOCK + x_ * CHIP + c_ * NARROW, 128), WIDE)

    mine = window(y, x, c)
    in_local = pltpu.make_async_copy(local_h.at[0], local_v, in_sem.at[0])
    in_base = pltpu.make_async_copy(base_h, base_v, in_sem.at[1])
    in_mom = pltpu.make_async_copy(mom_h.at[:, mine], mom_v, in_sem.at[2])
    in_local.start()
    in_base.start()
    in_mom.start()
    in_local.wait()
    in_base.wait()

    for k, (dx, dy, dc) in enumerate(PLANE):
        dev = (x + dx) % NX, (y + dy) % NY, (c + dc) % 2
        cols = window(dev[1], dev[0], dev[2])
        send1[k] = (base_v[:, cols].astype(f32) - local_v[:, cols].astype(f32)).astype(bf16)
        if k == 0:
            pl.semaphore_wait(barrier, len(PLANE) - 1 + NZ - 1)
        if k < 63:
            remote(send1.at[k], recv1.at[k], s1, r1.at[k // 32], at(*dev, z))
    total = send1[63].astype(f32)
    in_mom.wait()
    b = base_v[:, mine].astype(f32)
    for part in (range(32), range(32, 63)):
        drain(recv1.at[pl.ds(0, len(part))], r1.at[part[0] // 32])
        for k in part:
            total += recv1[k].astype(f32)
    grad = total * (1.0 / 64.0)
    new_m = 0.9 * mom_v[...] + grad
    new_b = (b - 0.7 * (grad + 0.9 * new_m)).astype(bf16)
    own_a[...] = new_b[:, :256]
    own_c[...] = new_b[:, 384:]
    abuf[z] = new_b[:, :256]
    bbuf[z, x, 0] = new_b[:, 256:384]
    cbuf[z, x] = new_b[:, 384:]
    for k in (2, 1, 3):
        remote(own_c, cbuf.at[z, x], sx_c, rx_c, x_peer(k))
    for k in SLOTS[:0:-1]:
        remote(own_a, abuf.at[z], sz_a, rz_a, z_peer(k))
        remote(bbuf.at[z, x, 0], bbuf.at[z, x, slot_of(-k)], sy_b, ry_b, y_peer(k))

    def rows(parts):
        return jnp.concatenate([p.astype(f32) for p in parts], axis=0).astype(bf16)

    def gather(par):
        lo, w = (0, WIDE) if par == 0 else (128, NARROW)
        other = WIDE + NARROW - w
        w_a = 256 - lo
        own = pl.ds(par * WIDE, w)
        cols = (pl.ds(par * WIDE, w_a), pl.ds(par * WIDE + w_a, 128), pl.ds(par * WIDE + w_a + 128, 128))

        def blocks(i, x_):
            return gath.at[pl.ds(*GROUPS[i]), x_, :, cols[0]]

        def halves(i, d, x_):
            return gath.at[pl.ds(*GROUPS[i]), x_, pl.ds(d * 16, 16), cols[0]]

        def pass_on(i, x_, k):
            remote(blocks(i, x_), blocks(i, x_), sc, rc.at[k, i], partner)

        def feed(i):
            if i in DIRECT:
                remote(blocks(i, x), blocks(i, x), sx, rf.at[i], x_peer(2))
            for d, k in enumerate((1, -1)):
                remote(blocks(i, x), blocks(i, x), sx, rx.at[d, i], x_peer(k))
            pass_on(i, x, 0)

        def take(i):
            for d, k in enumerate((1, -1)):
                from_ = (x - k) % NX
                drain(blocks(i, 0), rx.at[d, i])
                if i not in DIRECT:
                    remote(halves(i, d, from_), halves(i, d, from_), sx, rh.at[d, i], x_peer(k))
                pass_on(i, from_, 1 + d)

        def far(i):
            if i in DIRECT:
                drain(blocks(i, 0), rf.at[i])
            else:
                for d in range(2):
                    drain(halves(i, d, 0), rh.at[d, i])
            pass_on(i, (x + 2) % NX, 3)

        def momentum(x_):
            return gath_m.at[:, x_, :, own]

        gath_m[0, x, :, own] = new_m[:, lo:]
        for k in SLOTS[:0:-1]:
            remote(gath_m.at[0, x, :, own], gath_m.at[slot_of(-k), x, :, own], sy_m, ry_m, y_peer(k))
        drain(cbuf.at[0, pl.ds(0, 3)], rx_c)
        for k in SLOTS[:0:-1]:
            remote(cbuf.at[z], cbuf.at[z], sz_c, rz_c, z_peer(k))
        drain(bbuf.at[0, 0, pl.ds(0, 7)], ry_b)
        for k in (2, 1, 3):
            remote(bbuf.at[z, x], bbuf.at[z, x], sx_b, rx_b, x_peer(k))
        drain(abuf.at[pl.ds(0, 7)], rz_a)
        gath[0, x, :, cols[0]] = rows([abuf[i][:, lo:] for i in range(NZ)])
        for k in SLOTS[1:]:
            slot = slot_of(-k)
            group = max(i for i in range(len(GROUPS)) if GROUPS[i][0] <= slot)
            remote(gath.at[0, x, :, cols[0]], gath.at[slot, x, :, cols[0]], sy_a, ry_a.at[group - 1], y_peer(k))
        feed(0)
        drain(gath_m.at[pl.ds(0, 7), 0, :, own], ry_m)
        for k in (2, 1, 3):
            remote(momentum(x), momentum(x), sx_m, rx_m.at[k - 1], x_peer(k))
        remote(momentum(x), momentum(x), sc_m, rc_m.at[0], partner)
        drain(bbuf.at[0, pl.ds(0, 3)], rx_b)
        for k in SLOTS[:0:-1]:
            remote(bbuf.at[z], bbuf.at[z], sz_b, rz_b, z_peer(k))
        drain(cbuf.at[pl.ds(0, 7)], rz_c)
        for i in range(NX):
            gath[0, i, :, cols[2]] = rows([cbuf[j, i] for j in range(NZ)])
        for k in SLOTS[:0:-1]:
            slot = slot_of(-k)
            remote(gath.at[0, :, :, cols[2]], gath.at[slot, :, :, cols[2]], sy_c, ry_c.at[int(slot > 4)], y_peer(k))

        def pass_all(slots, part_, recv):
            block = gath.at[pl.ds(*slots), :, :, cols[part_]]
            remote(block, block, sc, recv, partner)

        def pass_c(i, slots):
            drain(gath.at[pl.ds(*slots), :, :, cols[2]], ry_c.at[i])
            pass_all(slots, 2, rc_c.at[1 + i])

        pass_all((0, 1), 2, rc_c.at[0])
        for i in range(1, len(GROUPS)):
            drain(blocks(i, 0), ry_a.at[i - 1])
            feed(i)
            take(i - 1)
        for k in (1, 3, 2):
            drain(momentum(0), rx_m.at[k - 1])
            remote(momentum((x - k) % NX), momentum((x - k) % NX), sc_m, rc_m.at[k], partner)
        for i in range(len(GROUPS) - 2):
            far(i)
        take(len(GROUPS) - 1)
        pass_c(0, (1, 4))
        far(len(GROUPS) - 2)
        drain(bbuf.at[pl.ds(0, 7)], rz_b)
        for s in range(NY):
            for i in range(NX):
                gath[s, i, :, cols[1]] = rows([bbuf[j, i, s] for j in range(NZ)])
            if s % 4 == 3:
                pass_all((s - 3, 4), 1, rc_b.at[s // 4])
        pass_c(1, (5, 3))
        far(len(GROUPS) - 1)
        drain(gath_m.at[pl.ds(0, 7), 0, :, own], sy_m)
        drain(gath.at[pl.ds(0, 7), 0, :, cols[0]], sy_a)
        drain(gath.at[pl.ds(0, 7), :, :, cols[2]], sy_c)
        drain(gath_m.at[:, pl.ds(0, 3), :, own], sx_m)
        drain(gath_m.at[:, :, :, own], sc_m)
        drain(gath.at[:, pl.ds(0, 3), :, cols[0]], sx)
        drain(gath.at[:, :, :, own], sc)
        for k in range(4):
            drain(gath_m.at[:, 0, :, pl.ds(0, other)], rc_m.at[k])
            for i, group in enumerate(GROUPS):
                drain(gath.at[pl.ds(*group), 0, :, pl.ds(0, other - 256)], rc.at[k, i])
        for i in range(2):
            drain(gath.at[pl.ds(0, 4), :, :, pl.ds(0, 128)], rc_b.at[i])
        for i, n in enumerate((1, 4, 3)):
            drain(gath.at[pl.ds(0, n), :, :, pl.ds(0, 128)], rc_c.at[i])

    for par in range(2):
        pl.when(c == par)(lambda par=par: gather(par))
    drain(recv1, s1)
    drain(abuf.at[pl.ds(0, 7)], sz_a)
    drain(bbuf.at[0, 0, pl.ds(0, 7)], sy_b)
    drain(bbuf.at[0, pl.ds(0, 3)], sx_b)
    drain(bbuf.at[pl.ds(0, 7)], sz_b)
    drain(cbuf.at[0, pl.ds(0, 3)], sx_c)
    drain(cbuf.at[pl.ds(0, 7)], sz_c)


def flush_kernel(gath, gath_m, newb, newm, sem):
    y = place()[1]
    copies = []
    for s, off in enumerate(SLOTS):
        for i in range(NX):
            cols = pl.ds(pl.multiple_of((y + off) % NY * BLOCK + i * CHIP, 128), CHIP)
            copies.append(pltpu.make_async_copy(gath.at[s, i], newb.at[:, cols], sem.at[0, s, i]))
            copies.append(pltpu.make_async_copy(gath_m.at[s, i], newm.at[:, cols], sem.at[1, s, i]))
    for copy in copies:
        copy.start()
    for copy in copies:
        copy.wait()


def shards(base_weight, local_weight, momentum):
    hbm, vmem = pl.BlockSpec(memory_space=pltpu.HBM), pl.BlockSpec(memory_space=pltpu.VMEM)
    dma, n = pltpu.SemaphoreType.DMA, len(GROUPS)
    gath, gath_m = pl.pallas_call(
        kernel,
        out_shape=(pltpu.VMEM((NY, NX, 32, CHIP), bf16), pltpu.VMEM((NY, NX, 4, CHIP), f32)),
        in_specs=[hbm] * 3,
        out_specs=(vmem, vmem),
        scratch_shapes=[
            pltpu.VMEM((4, FF), bf16),
            pltpu.VMEM((4, FF), bf16),
            pltpu.VMEM((4, WIDE), f32),
            pltpu.VMEM((64, 4, WIDE), bf16),
            pltpu.VMEM((63, 4, WIDE), bf16),
            pltpu.VMEM((4, 256), bf16),
            pltpu.VMEM((4, 128), bf16),
            pltpu.VMEM((NZ, 4, 256), bf16),
            pltpu.VMEM((NZ, NX, NY, 4, 128), bf16),
            pltpu.VMEM((NZ, NX, 4, 128), bf16),
            dma((3,)),
            dma((14,)),
            dma((2,)), dma, dma((n,)), dma, dma, dma, dma, dma, dma((2,)), dma, dma((3,)),
            dma((2, n)), dma((2, n)), dma((n,)), dma((4, n)), dma((2,)), dma((3,)), dma((4,)),
        ],
        compiler_params=pltpu.CompilerParams(collective_id=0, has_side_effects=True, vmem_limit_bytes=32 * 2**20),
        cost_estimate=pl.CostEstimate(flops=4 * FF * 8, bytes_accessed=32 * FF * 4, transcendentals=0),
    )(*(pltpu.with_memory_space_constraint(a, pltpu.HBM) for a in (base_weight, local_weight, momentum)))
    return pl.pallas_call(
        flush_kernel,
        out_shape=(pltpu.HBM((32, FF), bf16), pltpu.HBM((4, FF), f32)),
        in_specs=[vmem, vmem],
        out_specs=(hbm, hbm),
        scratch_shapes=[dma((2, NY, NX))],
        cost_estimate=pl.CostEstimate(flops=0, bytes_accessed=32 * FF * 4, transcendentals=0),
    )(*(pltpu.with_memory_space_constraint(a, pltpu.VMEM) for a in (gath, gath_m)))


def solution(mesh):
    return jax.shard_map(
        shards,
        mesh=mesh,
        in_specs=(P("fsdp", None), P("rep", "fsdp", None), P("fsdp", None)),
        out_specs=(P(), P("fsdp", None)),
        check_vma=False,
    )
```

```python
import jax
import jax.numpy as jnp
from jax import lax
from jax.experimental import pallas as pl
from jax.experimental.pallas import tpu as pltpu
from jax.sharding import PartitionSpec as P

FF = 28672
NX, NY, NZ = 4, 8, 8
BLOCK = FF // NY
CHIP = BLOCK // NX
WIDE, NARROW = 512, 384
SLOTS = (0, 1, -1, 2, -2, 3, -3, 4)
GROUPS = ((0, 1), (1, 2), (3, 2), (5, 3))
DIRECT = (3,)
PLANE = sorted(((i, j, k) for i in range(NX) for j in range(NY) for k in range(2)),
               key=lambda d: (-min(d[0], NX - d[0]) - min(d[1], NY - d[1]), -d[2]))
f32, bf16 = jnp.float32, jnp.bfloat16
MESH = pl.DeviceIdType.MESH


def slot_of(offset):
    return SLOTS.index((offset + 3) % NY - 3)


def place():
    rep = lax.axis_index("rep")
    return rep // (2 * NY), (rep // 2) % NY, rep % 2, lax.axis_index("fsdp")


def kernel(base_h, local_h, mom_h, gath, gath_m, base_v, local_v, mom_v, send1, recv1, own_a, own_c, abuf, bbuf,
           cbuf, in_sem, send_sem, r1, rz_a, ry_a, ry_b, rx_b, rz_b, rx_c, rz_c, ry_c, ry_m, rx_m, rx, rh, rf, rc, rc_m):
    x, y, c, z = place()
    s1, s1_other, sz_a, sy_a, sy_b, sx_b, sz_b, sx_c, sz_c, sy_c, sy_m, sx_m, sx, sc, sc_m = (send_sem.at[i] for i in range(15))

    def at(x_, y_, c_, z_):
        return {"rep": (x_ * NY + y_) * 2 + c_, "fsdp": z_}

    def y_peer(k):
        return at(x, (y + k) % NY, c, z)

    def z_peer(k):
        return at(x, y, c, (z + k) % NZ)

    def x_peer(k):
        return at((x + k) % NX, y, c, z)

    partner = at(x, y, 1 - c, z)
    barrier = pltpu.get_barrier_semaphore()
    for dx, dy, dc in PLANE[:-1]:
        dev = at((x + dx) % NX, (y + dy) % NY, (c + dc) % 2, z)
        pl.semaphore_signal(barrier, inc=1, device_id=dev, device_id_type=MESH)
    for k in range(1, NZ):
        pl.semaphore_signal(barrier, inc=1, device_id=z_peer(k), device_id_type=MESH)

    def remote(src, dst, send, recv, dev):
        pltpu.make_async_remote_copy(src_ref=src, dst_ref=dst, send_sem=send, recv_sem=recv, device_id=dev,
                                     device_id_type=MESH).start()

    def drain(ref, sem):
        pltpu.make_async_copy(ref, ref, sem).wait()

    in_local = pltpu.make_async_copy(local_h.at[0], local_v, in_sem.at[0])
    in_base = pltpu.make_async_copy(base_h, base_v, in_sem.at[1])
    in_local.start()
    in_base.start()

    def rows(parts):
        return jnp.concatenate([p.astype(f32) for p in parts], axis=0).astype(bf16)

    def replicas(par):
        w, other = (WIDE, NARROW) if par == 0 else (NARROW, WIDE)
        w_a = w - 256
        own = pl.ds(par * WIDE, w)
        parts = (pl.ds(0, w_a), pl.ds(w_a, 128), pl.ds(w_a + 128, 128))
        cols = (pl.ds(par * WIDE, w_a), pl.ds(par * WIDE + w_a, 128), pl.ds(par * WIDE + w_a + 128, 128))

        def window(j, x_, core):
            return pl.ds(pl.multiple_of(j * BLOCK + x_ * CHIP + core * WIDE, 128), NARROW if core else WIDE)

        mine = window(y, x, par)
        in_mom = pltpu.make_async_copy(mom_h.at[:, mine], mom_v.at[:, pl.ds(0, w)], in_sem.at[2])
        in_mom.start()
        in_local.wait()
        in_base.wait()

        for k, (dx, dy, dc) in enumerate(PLANE):
            j, h, core = (y + dy) % NY, (x + dx) % NX, (par + dc) % 2
            there = window(j, h, core)
            part = pl.ds(0, there.size)
            send1[k, :, part] = (base_v[:, there].astype(f32) - local_v[:, there].astype(f32)).astype(bf16)
            if k == 0:
                pl.semaphore_wait(barrier, len(PLANE) - 1 + NZ - 1)
            if k < 63:
                remote(send1.at[k, :, part], recv1.at[k, :, part], s1_other if dc else s1, r1.at[k // 32], at(h, j, core, z))
        total = send1[63, :, pl.ds(0, w)].astype(f32)
        in_mom.wait()
        b = base_v[:, mine].astype(f32)
        for some in (range(32), range(32, 63)):
            drain(recv1.at[pl.ds(0, len(some)), :, pl.ds(0, w)], r1.at[some[0] // 32])
            for k in some:
                total += recv1[k, :, pl.ds(0, w)].astype(f32)
        grad = total * (1.0 / 64.0)
        new_m = 0.9 * mom_v[:, pl.ds(0, w)] + grad
        new_b = (b - 0.7 * (grad + 0.9 * new_m)).astype(bf16)
        own_a[:, parts[0]] = new_b[:, :w_a]
        abuf[z, :, parts[0]] = new_b[:, :w_a]
        bbuf[z, x, 0] = new_b[:, w_a:w_a + 128]
        own_c[...] = new_b[:, w_a + 128:]
        cbuf[z, x] = new_b[:, w_a + 128:]
        for k in (2, 1, 3):
            remote(own_c, cbuf.at[z, x], sx_c, rx_c, x_peer(k))
        for k in SLOTS[:0:-1]:
            remote(own_a.at[:, parts[0]], abuf.at[z, :, parts[0]], sz_a, rz_a, z_peer(k))
        for dx in (2, 1, 3, 0):
            for dy in SLOTS[::-1]:
                if dx or dy:
                    send, recv = (sx_b, rx_b) if dx else (sy_b, ry_b)
                    remote(bbuf.at[z, x, 0], bbuf.at[z, x, slot_of(-dy)], send, recv, at((x + dx) % NX, (y + dy) % NY, c, z))

        def blocks(i, x_):
            return gath.at[pl.ds(*GROUPS[i]), x_, :, cols[0]]

        def halves(i, d, x_):
            return gath.at[pl.ds(*GROUPS[i]), x_, pl.ds(d * 16, 16), cols[0]]

        def pass_on(i, x_):
            remote(blocks(i, x_), blocks(i, x_), sc, rc, partner)

        def feed(i):
            if i in DIRECT:
                remote(blocks(i, x), blocks(i, x), sx, rf.at[i], x_peer(2))
            for d, k in enumerate((1, -1)):
                remote(blocks(i, x), blocks(i, x), sx, rx.at[d, i], x_peer(k))
            pass_on(i, x)

        def take(i):
            for d, k in enumerate((1, -1)):
                from_ = (x - k) % NX
                drain(blocks(i, 0), rx.at[d, i])
                if i not in DIRECT:
                    remote(halves(i, d, from_), halves(i, d, from_), sx, rh.at[d, i], x_peer(k))
                pass_on(i, from_)

        def far(i):
            if i in DIRECT:
                drain(blocks(i, 0), rf.at[i])
            else:
                for d in range(2):
                    drain(halves(i, d, 0), rh.at[d, i])
            pass_on(i, (x + 2) % NX)

        def momentum(x_):
            return gath_m.at[:, x_, :, own]

        gath_m[0, x, :, own] = new_m
        for k in SLOTS[:0:-1]:
            remote(gath_m.at[0, x, :, own], gath_m.at[slot_of(-k), x, :, own], sy_m, ry_m, y_peer(k))
        drain(cbuf.at[0, pl.ds(0, 3)], rx_c)
        for k in SLOTS[:0:-1]:
            remote(cbuf.at[z], cbuf.at[z], sz_c, rz_c, z_peer(k))
        drain(abuf.at[pl.ds(0, 7), :, parts[0]], rz_a)
        gath[0, x, :, cols[0]] = rows([abuf[i, :, parts[0]] for i in range(NZ)])
        for k in SLOTS[1:]:
            slot = slot_of(-k)
            group = max(i for i in range(len(GROUPS)) if GROUPS[i][0] <= slot)
            remote(gath.at[0, x, :, cols[0]], gath.at[slot, x, :, cols[0]], sy_a, ry_a.at[group - 1], y_peer(k))
        feed(0)
        drain(bbuf.at[0, 0, pl.ds(0, 7)], ry_b)
        drain(bbuf.at[0, pl.ds(0, 3)], rx_b)
        for k in SLOTS[:0:-1]:
            remote(bbuf.at[z], bbuf.at[z], sz_b, rz_b, z_peer(k))
        drain(gath_m.at[pl.ds(0, 7), 0, :, own], ry_m)
        for k in (2, 1, 3):
            remote(momentum(x), momentum(x), sx_m, rx_m.at[k - 1], x_peer(k))
        remote(momentum(x), momentum(x), sc_m, rc_m, partner)
        drain(cbuf.at[pl.ds(0, 7)], rz_c)
        for i in range(NX):
            gath[0, i, :, cols[2]] = rows([cbuf[j, i] for j in range(NZ)])
        for k in SLOTS[:0:-1]:
            slot = slot_of(-k)
            remote(gath.at[0, :, :, cols[2]], gath.at[slot, :, :, cols[2]], sy_c, ry_c.at[int(slot > 4)], y_peer(k))

        def pass_all(slots, part_):
            block = gath.at[pl.ds(*slots), :, :, cols[part_]]
            remote(block, block, sc, rc, partner)

        def pass_c(i, slots):
            drain(gath.at[pl.ds(*slots), :, :, cols[2]], ry_c.at[i])
            pass_all(slots, 2)

        pass_all((0, 1), 2)
        for i in range(1, len(GROUPS)):
            drain(blocks(i, 0), ry_a.at[i - 1])
            feed(i)
            take(i - 1)
        for k in (1, 3, 2):
            drain(momentum(0), rx_m.at[k - 1])
            remote(momentum((x - k) % NX), momentum((x - k) % NX), sc_m, rc_m, partner)
        for i in range(len(GROUPS) - 2):
            far(i)
        take(len(GROUPS) - 1)
        pass_c(0, (1, 4))
        far(len(GROUPS) - 2)
        drain(gath_m.at[pl.ds(0, 7), 0, :, own], sy_m)
        drain(gath.at[pl.ds(0, 7), 0, :, cols[0]], sy_a)
        drain(gath_m.at[:, pl.ds(0, 3), :, own], sx_m)
        drain(recv1.at[pl.ds(0, 31), :, pl.ds(0, w)], s1)
        drain(recv1.at[pl.ds(0, 32), :, pl.ds(0, other)], s1_other)
        drain(abuf.at[pl.ds(0, 7), :, parts[0]], sz_a)
        drain(bbuf.at[0, 0, pl.ds(0, 7)], sy_b)
        drain(bbuf.at[0, pl.ds(0, 3)], sx_b)
        drain(cbuf.at[0, pl.ds(0, 3)], sx_c)
        drain(cbuf.at[pl.ds(0, 7)], sz_c)
        drain(bbuf.at[pl.ds(0, 7)], rz_b)
        for s in range(NY):
            for i in range(NX):
                gath[s, i, :, cols[1]] = rows([bbuf[j, i, s] for j in range(NZ)])
            if s % 2 == 1:
                pass_all((s - 1, 2), 1)
        pass_c(1, (5, 3))
        far(len(GROUPS) - 1)
        drain(gath.at[pl.ds(0, 7), :, :, cols[2]], sy_c)
        drain(gath.at[:, pl.ds(0, 3), :, cols[0]], sx)
        drain(bbuf.at[pl.ds(0, 7)], sz_b)
        drain(gath_m.at[:, :, :, own], sc_m)
        drain(gath.at[:, :, :, own], sc)
        theirs = pl.ds((1 - par) * WIDE, other)
        drain(gath_m.at[:, :, :, theirs], rc_m)
        drain(gath.at[:, :, :, theirs], rc)

    for par in range(2):
        pl.when(c == par)(lambda par=par: replicas(par))


def flush_kernel(gath, gath_m, newb, newm, sem):
    y = place()[1]
    for s, off in enumerate(SLOTS):
        for i in range(NX):
            cols = pl.ds(pl.multiple_of((y + off) % NY * BLOCK + i * CHIP, 128), CHIP)
            pltpu.make_async_copy(gath.at[s, i], newb.at[:, cols], sem.at[0]).start()
            pltpu.make_async_copy(gath_m.at[s, i], newm.at[:, cols], sem.at[1]).start()
    pltpu.make_async_copy(newb, newb, sem.at[0]).wait()
    pltpu.make_async_copy(newm, newm, sem.at[1]).wait()


def shards(base_weight, local_weight, momentum):
    hbm, vmem = pl.BlockSpec(memory_space=pltpu.HBM), pl.BlockSpec(memory_space=pltpu.VMEM)
    dma, n = pltpu.SemaphoreType.DMA, len(GROUPS)
    gath, gath_m = pl.pallas_call(
        kernel,
        out_shape=(pltpu.VMEM((NY, NX, 32, CHIP), bf16), pltpu.VMEM((NY, NX, 4, CHIP), f32)),
        in_specs=[hbm] * 3,
        out_specs=(vmem, vmem),
        scratch_shapes=[
            pltpu.VMEM((4, FF), bf16),
            pltpu.VMEM((4, FF), bf16),
            pltpu.VMEM((4, WIDE), f32),
            pltpu.VMEM((64, 4, WIDE), bf16),
            pltpu.VMEM((63, 4, WIDE), bf16),
            pltpu.VMEM((4, 256), bf16),
            pltpu.VMEM((4, 128), bf16),
            pltpu.VMEM((NZ, 4, 256), bf16),
            pltpu.VMEM((NZ, NX, NY, 4, 128), bf16),
            pltpu.VMEM((NZ, NX, 4, 128), bf16),
            dma((3,)),
            dma((15,)),
            dma((2,)), dma, dma((n,)), dma, dma, dma, dma, dma, dma((2,)), dma, dma((3,)),
            dma((2, n)), dma((2, n)), dma((n,)), dma, dma,
        ],
        compiler_params=pltpu.CompilerParams(collective_id=0, has_side_effects=True, vmem_limit_bytes=32 * 2**20),
        cost_estimate=pl.CostEstimate(flops=4 * FF * 8, bytes_accessed=32 * FF * 4, transcendentals=0),
    )(*(pltpu.with_memory_space_constraint(a, pltpu.HBM) for a in (base_weight, local_weight, momentum)))
    return pl.pallas_call(
        flush_kernel,
        out_shape=(pltpu.HBM((32, FF), bf16), pltpu.HBM((4, FF), f32)),
        in_specs=[vmem, vmem],
        out_specs=(hbm, hbm),
        scratch_shapes=[dma((2,))],
        cost_estimate=pl.CostEstimate(flops=0, bytes_accessed=32 * FF * 4, transcendentals=0),
    )(*(pltpu.with_memory_space_constraint(a, pltpu.VMEM) for a in (gath, gath_m)))


def solution(mesh):
    return jax.shard_map(
        shards,
        mesh=mesh,
        in_specs=(P("fsdp", None), P("rep", "fsdp", None), P("fsdp", None)),
        out_specs=(P(), P("fsdp", None)),
        check_vma=False,
    )
```

```python
import jax
import jax.numpy as jnp
from jax import lax
from jax.experimental import pallas as pl
from jax.experimental.pallas import tpu as pltpu
from jax.sharding import PartitionSpec as P

FF = 28672
NX, NY, NZ = 4, 8, 8
BLOCK = FF // NY
CHIP = BLOCK // NX
WIDE, NARROW = 512, 384
SLOTS = (0, 1, -1, 2, -2, 3, -3, 4)
GROUPS = ((0, 1), (1, 4), (5, 3))
DIRECT = (1, 2)
PLANE = sorted(((i, j, k) for i in range(NX) for j in range(NY) for k in range(2)),
               key=lambda d: (-min(d[0], NX - d[0]) - min(d[1], NY - d[1]), -d[2]))
f32, bf16 = jnp.float32, jnp.bfloat16
MESH = pl.DeviceIdType.MESH


def slot_of(offset):
    return SLOTS.index((offset + 3) % NY - 3)


def place():
    rep = lax.axis_index("rep")
    return rep // (2 * NY), (rep // 2) % NY, rep % 2, lax.axis_index("fsdp")


def kernel(base_h, local_h, mom_h, gath, gath_m, base_v, local_v, mom_v, send1, recv1, own_a, own_c, abuf, bbuf,
           cbuf, in_sem, send_sem, r1, rz_a, ry_a, ry_b, rx_b, rz_b, rx_c, rz_c, ry_c, ry_m, rx_m, rx, rh, rf, rc, rc_m):
    x, y, c, z = place()
    s1, s1_other, sz_a, sy_a, sy_b, sx_b, sz_b, sx_c, sz_c, sy_c, sy_m, sx_m, sx, sc, sc_m = (send_sem.at[i] for i in range(15))

    def at(x_, y_, c_, z_):
        return {"rep": (x_ * NY + y_) * 2 + c_, "fsdp": z_}

    def y_peer(k):
        return at(x, (y + k) % NY, c, z)

    def z_peer(k):
        return at(x, y, c, (z + k) % NZ)

    def x_peer(k):
        return at((x + k) % NX, y, c, z)

    partner = at(x, y, 1 - c, z)
    barrier = pltpu.get_barrier_semaphore()
    for dx, dy, dc in PLANE[:-1]:
        dev = at((x + dx) % NX, (y + dy) % NY, (c + dc) % 2, z)
        pl.semaphore_signal(barrier, inc=1, device_id=dev, device_id_type=MESH)
    for k in range(1, NZ):
        pl.semaphore_signal(barrier, inc=1, device_id=z_peer(k), device_id_type=MESH)

    def remote(src, dst, send, recv, dev):
        pltpu.make_async_remote_copy(src_ref=src, dst_ref=dst, send_sem=send, recv_sem=recv, device_id=dev,
                                     device_id_type=MESH).start()

    def drain(ref, sem):
        pltpu.make_async_copy(ref, ref, sem).wait()

    in_local = pltpu.make_async_copy(local_h.at[0], local_v, in_sem.at[0])
    in_base = pltpu.make_async_copy(base_h, base_v, in_sem.at[1])
    in_local.start()
    in_base.start()

    def rows(parts):
        return jnp.concatenate([p.astype(f32) for p in parts], axis=0).astype(bf16)

    def replicas(par):
        w, other = (WIDE, NARROW) if par == 0 else (NARROW, WIDE)
        w_a = w - 256
        own = pl.ds(par * WIDE, w)
        parts = (pl.ds(0, w_a), pl.ds(w_a, 128), pl.ds(w_a + 128, 128))
        cols = (pl.ds(par * WIDE, w_a), pl.ds(par * WIDE + w_a, 128), pl.ds(par * WIDE + w_a + 128, 128))

        def window(j, x_, core):
            return pl.ds(pl.multiple_of(j * BLOCK + x_ * CHIP + core * WIDE, 128), NARROW if core else WIDE)

        mine = window(y, x, par)
        in_mom = pltpu.make_async_copy(mom_h.at[:, mine], mom_v.at[:, pl.ds(0, w)], in_sem.at[2])
        in_mom.start()
        in_local.wait()
        in_base.wait()

        for k, (dx, dy, dc) in enumerate(PLANE):
            j, h, core = (y + dy) % NY, (x + dx) % NX, (par + dc) % 2
            there = window(j, h, core)
            part = pl.ds(0, there.size)
            send1[k, :, part] = (base_v[:, there].astype(f32) - local_v[:, there].astype(f32)).astype(bf16)
            if k == 0:
                pl.semaphore_wait(barrier, len(PLANE) - 1 + NZ - 1)
            if k < 63:
                remote(send1.at[k, :, part], recv1.at[k, :, part], s1_other if dc else s1, r1.at[k // 32], at(h, j, core, z))
        total = send1[63, :, pl.ds(0, w)].astype(f32)
        in_mom.wait()
        b = base_v[:, mine].astype(f32)
        for some in (range(32), range(32, 63)):
            drain(recv1.at[pl.ds(0, len(some)), :, pl.ds(0, w)], r1.at[some[0] // 32])
            for k in some:
                total += recv1[k, :, pl.ds(0, w)].astype(f32)
        grad = total * (1.0 / 64.0)
        new_m = 0.9 * mom_v[:, pl.ds(0, w)] + grad
        new_b = (b - 0.7 * (grad + 0.9 * new_m)).astype(bf16)
        own_a[:, parts[0]] = new_b[:, :w_a]
        abuf[z, :, parts[0]] = new_b[:, :w_a]
        bbuf[z, x, 0] = new_b[:, w_a:w_a + 128]
        own_c[...] = new_b[:, w_a + 128:]
        cbuf[z, x] = new_b[:, w_a + 128:]
        for k in SLOTS[:0:-1]:
            remote(own_a.at[:, parts[0]], abuf.at[z, :, parts[0]], sz_a, rz_a, z_peer(k))
        for k in (2, 1, 3):
            remote(own_c, cbuf.at[z, x], sx_c, rx_c, x_peer(k))
        for dx in (2, 1, 3, 0):
            for dy in SLOTS[::-1]:
                if dx or dy:
                    send, recv = (sx_b, rx_b) if dx else (sy_b, ry_b)
                    remote(bbuf.at[z, x, 0], bbuf.at[z, x, slot_of(-dy)], send, recv, at((x + dx) % NX, (y + dy) % NY, c, z))

        def blocks(i, x_):
            return gath.at[pl.ds(*GROUPS[i]), x_, :, cols[0]]

        def halves(i, d, x_):
            return gath.at[pl.ds(*GROUPS[i]), x_, pl.ds(d * 16, 16), cols[0]]

        def pass_on(i, x_):
            remote(blocks(i, x_), blocks(i, x_), sc, rc, partner)

        def feed(i):
            if i in DIRECT:
                remote(blocks(i, x), blocks(i, x), sx, rf.at[i], x_peer(2))
            for d, k in enumerate((1, -1)):
                remote(blocks(i, x), blocks(i, x), sx, rx.at[d, i], x_peer(k))
            pass_on(i, x)

        def take(i):
            for d, k in enumerate((1, -1)):
                from_ = (x - k) % NX
                drain(blocks(i, 0), rx.at[d, i])
                if i not in DIRECT:
                    remote(halves(i, d, from_), halves(i, d, from_), sx, rh.at[d, i], x_peer(k))
                pass_on(i, from_)

        def far(i):
            if i in DIRECT:
                drain(blocks(i, 0), rf.at[i])
            else:
                for d in range(2):
                    drain(halves(i, d, 0), rh.at[d, i])
            pass_on(i, (x + 2) % NX)

        def momentum(x_):
            return gath_m.at[:, x_, :, own]

        gath_m[0, x, :, own] = new_m
        for k in SLOTS[:0:-1]:
            remote(gath_m.at[0, x, :, own], gath_m.at[slot_of(-k), x, :, own], sy_m, ry_m, y_peer(k))
        drain(cbuf.at[0, pl.ds(0, 3)], rx_c)
        for k in SLOTS[:0:-1]:
            remote(cbuf.at[z], cbuf.at[z], sz_c, rz_c, z_peer(k))
        drain(abuf.at[pl.ds(0, 7), :, parts[0]], rz_a)
        gath[0, x, :, cols[0]] = rows([abuf[i, :, parts[0]] for i in range(NZ)])
        for k in SLOTS[1:]:
            slot = slot_of(-k)
            group = max(i for i in range(len(GROUPS)) if GROUPS[i][0] <= slot)
            remote(gath.at[0, x, :, cols[0]], gath.at[slot, x, :, cols[0]], sy_a, ry_a.at[group - 1], y_peer(k))
        feed(0)
        drain(bbuf.at[0, 0, pl.ds(0, 7)], ry_b)
        drain(bbuf.at[0, pl.ds(0, 3)], rx_b)
        for k in SLOTS[:0:-1]:
            remote(bbuf.at[z], bbuf.at[z], sz_b, rz_b, z_peer(k))
        drain(gath_m.at[pl.ds(0, 7), 0, :, own], ry_m)
        for k in (2, 1, 3):
            remote(momentum(x), momentum(x), sx_m, rx_m.at[k - 1], x_peer(k))
        remote(momentum(x), momentum(x), sc_m, rc_m, partner)
        drain(cbuf.at[pl.ds(0, 7)], rz_c)
        for i in range(NX):
            gath[0, i, :, cols[2]] = rows([cbuf[j, i] for j in range(NZ)])
        for k in SLOTS[:0:-1]:
            slot = slot_of(-k)
            remote(gath.at[0, :, :, cols[2]], gath.at[slot, :, :, cols[2]], sy_c, ry_c.at[int(slot > 4)], y_peer(k))

        def pass_all(slots, part_):
            block = gath.at[pl.ds(*slots), :, :, cols[part_]]
            remote(block, block, sc, rc, partner)

        def pass_c(i, slots):
            drain(gath.at[pl.ds(*slots), :, :, cols[2]], ry_c.at[i])
            pass_all(slots, 2)

        pass_all((0, 1), 2)
        for i in range(1, len(GROUPS)):
            drain(blocks(i, 0), ry_a.at[i - 1])
            feed(i)
            take(i - 1)
        for k in (1, 3, 2):
            drain(momentum(0), rx_m.at[k - 1])
            remote(momentum((x - k) % NX), momentum((x - k) % NX), sc_m, rc_m, partner)
        for i in range(len(GROUPS) - 2):
            far(i)
        drain(gath_m.at[pl.ds(0, 7), 0, :, own], sy_m)
        drain(gath.at[pl.ds(0, 7), 0, :, cols[0]], sy_a)
        drain(gath_m.at[:, pl.ds(0, 3), :, own], sx_m)
        drain(recv1.at[pl.ds(0, 31), :, pl.ds(0, w)], s1)
        drain(recv1.at[pl.ds(0, 32), :, pl.ds(0, other)], s1_other)
        drain(abuf.at[pl.ds(0, 7), :, parts[0]], sz_a)
        drain(bbuf.at[0, 0, pl.ds(0, 7)], sy_b)
        drain(bbuf.at[0, pl.ds(0, 3)], sx_b)
        drain(cbuf.at[0, pl.ds(0, 3)], sx_c)
        drain(cbuf.at[pl.ds(0, 7)], sz_c)
        drain(bbuf.at[pl.ds(0, 7)], rz_b)
        for s in range(NY):
            for i in range(NX):
                gath[s, i, :, cols[1]] = rows([bbuf[j, i, s] for j in range(NZ)])
            if s % 2 == 1:
                pass_all((s - 1, 2), 1)
        take(len(GROUPS) - 1)
        pass_c(0, (1, 4))
        far(len(GROUPS) - 2)
        pass_c(1, (5, 3))
        far(len(GROUPS) - 1)
        drain(gath.at[pl.ds(0, 7), :, :, cols[2]], sy_c)
        drain(gath.at[:, pl.ds(0, 3), :, cols[0]], sx)
        drain(bbuf.at[pl.ds(0, 7)], sz_b)
        drain(gath_m.at[:, :, :, own], sc_m)
        drain(gath.at[:, :, :, own], sc)
        theirs = pl.ds((1 - par) * WIDE, other)
        drain(gath_m.at[:, :, :, theirs], rc_m)
        drain(gath.at[:, :, :, theirs], rc)

    for par in range(2):
        pl.when(c == par)(lambda par=par: replicas(par))


def flush_kernel(gath, gath_m, newb, newm, sem):
    y = place()[1]
    for s, off in enumerate(SLOTS):
        for i in range(NX):
            cols = pl.ds(pl.multiple_of((y + off) % NY * BLOCK + i * CHIP, 128), CHIP)
            pltpu.make_async_copy(gath.at[s, i], newb.at[:, cols], sem.at[0]).start()
            pltpu.make_async_copy(gath_m.at[s, i], newm.at[:, cols], sem.at[1]).start()
    pltpu.make_async_copy(newb, newb, sem.at[0]).wait()
    pltpu.make_async_copy(newm, newm, sem.at[1]).wait()


def shards(base_weight, local_weight, momentum):
    hbm, vmem = pl.BlockSpec(memory_space=pltpu.HBM), pl.BlockSpec(memory_space=pltpu.VMEM)
    dma, n = pltpu.SemaphoreType.DMA, len(GROUPS)
    gath, gath_m = pl.pallas_call(
        kernel,
        out_shape=(pltpu.VMEM((NY, NX, 32, CHIP), bf16), pltpu.VMEM((NY, NX, 4, CHIP), f32)),
        in_specs=[hbm] * 3,
        out_specs=(vmem, vmem),
        scratch_shapes=[
            pltpu.VMEM((4, FF), bf16),
            pltpu.VMEM((4, FF), bf16),
            pltpu.VMEM((4, WIDE), f32),
            pltpu.VMEM((64, 4, WIDE), bf16),
            pltpu.VMEM((63, 4, WIDE), bf16),
            pltpu.VMEM((4, 256), bf16),
            pltpu.VMEM((4, 128), bf16),
            pltpu.VMEM((NZ, 4, 256), bf16),
            pltpu.VMEM((NZ, NX, NY, 4, 128), bf16),
            pltpu.VMEM((NZ, NX, 4, 128), bf16),
            dma((3,)),
            dma((15,)),
            dma((2,)), dma, dma((n,)), dma, dma, dma, dma, dma, dma((2,)), dma, dma((3,)),
            dma((2, n)), dma((2, n)), dma((n,)), dma, dma,
        ],
        compiler_params=pltpu.CompilerParams(collective_id=0, has_side_effects=True, vmem_limit_bytes=32 * 2**20),
        cost_estimate=pl.CostEstimate(flops=4 * FF * 8, bytes_accessed=32 * FF * 4, transcendentals=0),
    )(*(pltpu.with_memory_space_constraint(a, pltpu.HBM) for a in (base_weight, local_weight, momentum)))
    return pl.pallas_call(
        flush_kernel,
        out_shape=(pltpu.HBM((32, FF), bf16), pltpu.HBM((4, FF), f32)),
        in_specs=[vmem, vmem],
        out_specs=(hbm, hbm),
        scratch_shapes=[dma((2,))],
        cost_estimate=pl.CostEstimate(flops=0, bytes_accessed=32 * FF * 4, transcendentals=0),
    )(*(pltpu.with_memory_space_constraint(a, pltpu.VMEM) for a in (gath, gath_m)))


def solution(mesh):
    return jax.shard_map(
        shards,
        mesh=mesh,
        in_specs=(P("fsdp", None), P("rep", "fsdp", None), P("fsdp", None)),
        out_specs=(P(), P("fsdp", None)),
        check_vma=False,
    )
```

```python
import jax
import jax.numpy as jnp
from jax import lax
from jax.experimental import pallas as pl
from jax.experimental.pallas import tpu as pltpu
from jax.sharding import PartitionSpec as P

FF = 28672
NX, NY, NZ = 4, 8, 8
BLOCK = FF // NY
CHIP = BLOCK // NX
WIDE, NARROW = 512, 384
SLOTS = (0, 1, -1, 2, -2, 3, -3, 4)
GROUPS = ((0, 1), (1, 4), (5, 3))
DIRECT = (0, 1, 2)
PLANE = sorted(((i, j, k) for i in range(NX) for j in range(NY) for k in range(2)),
               key=lambda d: (-min(d[0], NX - d[0]) - min(d[1], NY - d[1]), -d[2]))
f32, bf16 = jnp.float32, jnp.bfloat16
MESH = pl.DeviceIdType.MESH


def slot_of(offset):
    return SLOTS.index((offset + 3) % NY - 3)


def place():
    rep = lax.axis_index("rep")
    return rep // (2 * NY), (rep // 2) % NY, rep % 2, lax.axis_index("fsdp")


def kernel(base_h, local_h, mom_h, gath, gath_m, base_v, local_v, mom_v, send1, recv1, own_a, own_c, abuf, bbuf,
           cbuf, in_sem, send_sem, r1, rz_a, ry_a, ry_b, rx_b, rz_b, rx_c, rz_c, ry_c, ry_m, rx_m, rx, rh, rf, rc, rc_m):
    x, y, c, z = place()
    s1, s1_other, sz_a, sy_a, sy_b, sx_b, sz_b, sx_c, sz_c, sy_c, sy_m, sx_m, sx, sc, sc_m = (send_sem.at[i] for i in range(15))

    def at(x_, y_, c_, z_):
        return {"rep": (x_ * NY + y_) * 2 + c_, "fsdp": z_}

    def y_peer(k):
        return at(x, (y + k) % NY, c, z)

    def z_peer(k):
        return at(x, y, c, (z + k) % NZ)

    def x_peer(k):
        return at((x + k) % NX, y, c, z)

    partner = at(x, y, 1 - c, z)
    barrier = pltpu.get_barrier_semaphore()
    for dx, dy, dc in PLANE[:-1]:
        dev = at((x + dx) % NX, (y + dy) % NY, (c + dc) % 2, z)
        pl.semaphore_signal(barrier, inc=1, device_id=dev, device_id_type=MESH)
    for k in range(1, NZ):
        pl.semaphore_signal(barrier, inc=1, device_id=z_peer(k), device_id_type=MESH)

    def remote(src, dst, send, recv, dev):
        pltpu.make_async_remote_copy(src_ref=src, dst_ref=dst, send_sem=send, recv_sem=recv, device_id=dev,
                                     device_id_type=MESH).start()

    def drain(ref, sem):
        pltpu.make_async_copy(ref, ref, sem).wait()

    in_local = pltpu.make_async_copy(local_h.at[0], local_v, in_sem.at[0])
    in_base = pltpu.make_async_copy(base_h, base_v, in_sem.at[1])
    in_local.start()
    in_base.start()

    def rows(parts):
        return jnp.concatenate([p.astype(f32) for p in parts], axis=0).astype(bf16)

    def replicas(par):
        w, other = (WIDE, NARROW) if par == 0 else (NARROW, WIDE)
        w_a = w - 256
        own = pl.ds(par * WIDE, w)
        parts = (pl.ds(0, w_a), pl.ds(w_a, 128), pl.ds(w_a + 128, 128))
        cols = (pl.ds(par * WIDE, w_a), pl.ds(par * WIDE + w_a, 128), pl.ds(par * WIDE + w_a + 128, 128))

        def window(j, x_, core):
            return pl.ds(pl.multiple_of(j * BLOCK + x_ * CHIP + core * WIDE, 128), NARROW if core else WIDE)

        mine = window(y, x, par)
        in_mom = pltpu.make_async_copy(mom_h.at[:, mine], mom_v.at[:, pl.ds(0, w)], in_sem.at[2])
        in_mom.start()
        in_local.wait()
        in_base.wait()

        for k, (dx, dy, dc) in enumerate(PLANE):
            j, h, core = (y + dy) % NY, (x + dx) % NX, (par + dc) % 2
            there = window(j, h, core)
            part = pl.ds(0, there.size)
            send1[k, :, part] = (base_v[:, there].astype(f32) - local_v[:, there].astype(f32)).astype(bf16)
            if k == 0:
                pl.semaphore_wait(barrier, len(PLANE) - 1 + NZ - 1)
            if k < 63:
                remote(send1.at[k, :, part], recv1.at[k, :, part], s1_other if dc else s1, r1.at[k // 32], at(h, j, core, z))
        total = send1[63, :, pl.ds(0, w)].astype(f32)
        in_mom.wait()
        b = base_v[:, mine].astype(f32)
        for some in (range(32), range(32, 63)):
            drain(recv1.at[pl.ds(0, len(some)), :, pl.ds(0, w)], r1.at[some[0] // 32])
            for k in some:
                total += recv1[k, :, pl.ds(0, w)].astype(f32)
        grad = total * (1.0 / 64.0)
        new_m = 0.9 * mom_v[:, pl.ds(0, w)] + grad
        new_b = (b - 0.7 * (grad + 0.9 * new_m)).astype(bf16)
        own_a[:, parts[0]] = new_b[:, :w_a]
        abuf[z, :, parts[0]] = new_b[:, :w_a]
        bbuf[z, x, 0] = new_b[:, w_a:w_a + 128]
        own_c[...] = new_b[:, w_a + 128:]
        cbuf[z, x] = new_b[:, w_a + 128:]
        for k in SLOTS[:0:-1]:
            remote(own_a.at[:, parts[0]], abuf.at[z, :, parts[0]], sz_a, rz_a, z_peer(k))
        for k in (2, 1, 3):
            remote(own_c, cbuf.at[z, x], sx_c, rx_c, x_peer(k))
        for dx in (2, 1, 3, 0):
            for dy in SLOTS[::-1]:
                if dx or dy:
                    send, recv = (sx_b, rx_b) if dx else (sy_b, ry_b)
                    remote(bbuf.at[z, x, 0], bbuf.at[z, x, slot_of(-dy)], send, recv, at((x + dx) % NX, (y + dy) % NY, c, z))

        def blocks(i, x_):
            return gath.at[pl.ds(*GROUPS[i]), x_, :, cols[0]]

        def halves(i, d, x_):
            return gath.at[pl.ds(*GROUPS[i]), x_, pl.ds(d * 16, 16), cols[0]]

        def pass_on(i, x_):
            remote(blocks(i, x_), blocks(i, x_), sc, rc, partner)

        def feed(i):
            if i in DIRECT:
                remote(blocks(i, x), blocks(i, x), sx, rf.at[i], x_peer(2))
            for d, k in enumerate((1, -1)):
                remote(blocks(i, x), blocks(i, x), sx, rx.at[d, i], x_peer(k))
            pass_on(i, x)

        def take(i):
            for d, k in enumerate((1, -1)):
                from_ = (x - k) % NX
                drain(blocks(i, 0), rx.at[d, i])
                if i not in DIRECT:
                    remote(halves(i, d, from_), halves(i, d, from_), sx, rh.at[d, i], x_peer(k))
                pass_on(i, from_)

        def far(i):
            if i in DIRECT:
                drain(blocks(i, 0), rf.at[i])
            else:
                for d in range(2):
                    drain(halves(i, d, 0), rh.at[d, i])
            pass_on(i, (x + 2) % NX)

        def momentum(x_):
            return gath_m.at[:, x_, :, own]

        gath_m[0, x, :, own] = new_m
        for k in SLOTS[:0:-1]:
            remote(gath_m.at[0, x, :, own], gath_m.at[slot_of(-k), x, :, own], sy_m, ry_m, y_peer(k))
        drain(cbuf.at[0, pl.ds(0, 3)], rx_c)
        for k in SLOTS[:0:-1]:
            remote(cbuf.at[z], cbuf.at[z], sz_c, rz_c, z_peer(k))
        drain(abuf.at[pl.ds(0, 7), :, parts[0]], rz_a)
        gath[0, x, :, cols[0]] = rows([abuf[i, :, parts[0]] for i in range(NZ)])
        for k in SLOTS[1:]:
            slot = slot_of(-k)
            group = max(i for i in range(len(GROUPS)) if GROUPS[i][0] <= slot)
            remote(gath.at[0, x, :, cols[0]], gath.at[slot, x, :, cols[0]], sy_a, ry_a.at[group - 1], y_peer(k))
        feed(0)
        drain(bbuf.at[0, 0, pl.ds(0, 7)], ry_b)
        drain(bbuf.at[0, pl.ds(0, 3)], rx_b)
        for k in SLOTS[:0:-1]:
            remote(bbuf.at[z], bbuf.at[z], sz_b, rz_b, z_peer(k))
        drain(gath_m.at[pl.ds(0, 7), 0, :, own], ry_m)
        for k in (2, 1, 3):
            remote(momentum(x), momentum(x), sx_m, rx_m.at[k - 1], x_peer(k))
        remote(momentum(x), momentum(x), sc_m, rc_m, partner)
        drain(cbuf.at[pl.ds(0, 7)], rz_c)
        for i in range(NX):
            gath[0, i, :, cols[2]] = rows([cbuf[j, i] for j in range(NZ)])
        for k in SLOTS[:0:-1]:
            slot = slot_of(-k)
            remote(gath.at[0, :, :, cols[2]], gath.at[slot, :, :, cols[2]], sy_c, ry_c.at[int(slot > 4)], y_peer(k))

        def pass_all(slots, part_):
            block = gath.at[pl.ds(*slots), :, :, cols[part_]]
            remote(block, block, sc, rc, partner)

        def pass_c(i, slots):
            drain(gath.at[pl.ds(*slots), :, :, cols[2]], ry_c.at[i])
            pass_all(slots, 2)

        pass_all((0, 1), 2)
        for i in range(1, len(GROUPS)):
            drain(blocks(i, 0), ry_a.at[i - 1])
            feed(i)
            take(i - 1)
        for k in (1, 3, 2):
            drain(momentum(0), rx_m.at[k - 1])
            remote(momentum((x - k) % NX), momentum((x - k) % NX), sc_m, rc_m, partner)
        for i in range(len(GROUPS) - 2):
            far(i)
        drain(gath_m.at[pl.ds(0, 7), 0, :, own], sy_m)
        drain(gath.at[pl.ds(0, 7), 0, :, cols[0]], sy_a)
        drain(gath_m.at[:, pl.ds(0, 3), :, own], sx_m)
        drain(recv1.at[pl.ds(0, 31), :, pl.ds(0, w)], s1)
        drain(recv1.at[pl.ds(0, 32), :, pl.ds(0, other)], s1_other)
        drain(abuf.at[pl.ds(0, 7), :, parts[0]], sz_a)
        drain(bbuf.at[0, 0, pl.ds(0, 7)], sy_b)
        drain(bbuf.at[0, pl.ds(0, 3)], sx_b)
        drain(cbuf.at[0, pl.ds(0, 3)], sx_c)
        drain(cbuf.at[pl.ds(0, 7)], sz_c)
        drain(bbuf.at[pl.ds(0, 7)], rz_b)
        for s in range(NY):
            for i in range(NX):
                gath[s, i, :, cols[1]] = rows([bbuf[j, i, s] for j in range(NZ)])
            if s % 2 == 1:
                pass_all((s - 1, 2), 1)
        take(len(GROUPS) - 1)
        pass_c(0, (1, 4))
        far(len(GROUPS) - 2)
        pass_c(1, (5, 3))
        far(len(GROUPS) - 1)
        drain(gath.at[pl.ds(0, 7), :, :, cols[2]], sy_c)
        drain(gath.at[:, pl.ds(0, 3), :, cols[0]], sx)
        drain(bbuf.at[pl.ds(0, 7)], sz_b)
        drain(gath_m.at[:, :, :, own], sc_m)
        drain(gath.at[:, :, :, own], sc)
        theirs = pl.ds((1 - par) * WIDE, other)
        drain(gath_m.at[:, :, :, theirs], rc_m)
        drain(gath.at[:, :, :, theirs], rc)

    for par in range(2):
        pl.when(c == par)(lambda par=par: replicas(par))


def flush_kernel(gath, gath_m, newb, newm, sem):
    y = place()[1]
    for s, off in enumerate(SLOTS):
        for i in range(NX):
            cols = pl.ds(pl.multiple_of((y + off) % NY * BLOCK + i * CHIP, 128), CHIP)
            pltpu.make_async_copy(gath.at[s, i], newb.at[:, cols], sem.at[0]).start()
            pltpu.make_async_copy(gath_m.at[s, i], newm.at[:, cols], sem.at[1]).start()
    pltpu.make_async_copy(newb, newb, sem.at[0]).wait()
    pltpu.make_async_copy(newm, newm, sem.at[1]).wait()


def shards(base_weight, local_weight, momentum):
    hbm, vmem = pl.BlockSpec(memory_space=pltpu.HBM), pl.BlockSpec(memory_space=pltpu.VMEM)
    dma, n = pltpu.SemaphoreType.DMA, len(GROUPS)
    gath, gath_m = pl.pallas_call(
        kernel,
        out_shape=(pltpu.VMEM((NY, NX, 32, CHIP), bf16), pltpu.VMEM((NY, NX, 4, CHIP), f32)),
        in_specs=[hbm] * 3,
        out_specs=(vmem, vmem),
        scratch_shapes=[
            pltpu.VMEM((4, FF), bf16),
            pltpu.VMEM((4, FF), bf16),
            pltpu.VMEM((4, WIDE), f32),
            pltpu.VMEM((64, 4, WIDE), bf16),
            pltpu.VMEM((63, 4, WIDE), bf16),
            pltpu.VMEM((4, 256), bf16),
            pltpu.VMEM((4, 128), bf16),
            pltpu.VMEM((NZ, 4, 256), bf16),
            pltpu.VMEM((NZ, NX, NY, 4, 128), bf16),
            pltpu.VMEM((NZ, NX, 4, 128), bf16),
            dma((3,)),
            dma((15,)),
            dma((2,)), dma, dma((n,)), dma, dma, dma, dma, dma, dma((2,)), dma, dma((3,)),
            dma((2, n)), dma((2, n)), dma((n,)), dma, dma,
        ],
        compiler_params=pltpu.CompilerParams(collective_id=0, has_side_effects=True, vmem_limit_bytes=32 * 2**20),
        cost_estimate=pl.CostEstimate(flops=4 * FF * 8, bytes_accessed=32 * FF * 4, transcendentals=0),
    )(*(pltpu.with_memory_space_constraint(a, pltpu.HBM) for a in (base_weight, local_weight, momentum)))
    return pl.pallas_call(
        flush_kernel,
        out_shape=(pltpu.HBM((32, FF), bf16), pltpu.HBM((4, FF), f32)),
        in_specs=[vmem, vmem],
        out_specs=(hbm, hbm),
        scratch_shapes=[dma((2,))],
        cost_estimate=pl.CostEstimate(flops=0, bytes_accessed=32 * FF * 4, transcendentals=0),
    )(*(pltpu.with_memory_space_constraint(a, pltpu.VMEM) for a in (gath, gath_m)))


def solution(mesh):
    return jax.shard_map(
        shards,
        mesh=mesh,
        in_specs=(P("fsdp", None), P("rep", "fsdp", None), P("fsdp", None)),
        out_specs=(P(), P("fsdp", None)),
        check_vma=False,
    )
```
